256 devices in a mesh: section: 8 (over y, core), dp: 32 (over z, x).
Axes of the slice: x: 4, y: 4, z: 8, core: 2. Of those that a mesh axis runs over, the one named last changes fastest.
Arguments:
- hidden_in: bfloat16 [8, 4096, 5120], P('section', 'dp'), may hold values from -400 to 400
- norm_gain: bfloat16 [8, 5120], P('section', 'dp'), may hold values from 0.5 to 1.5
- key_weight: bfloat16 [8, 5120, 512], P('section', 'dp'), may hold values from -0.078125 to 0.078125
- value_weight: bfloat16 [8, 5120, 512], P('section', 'dp'), may hold values from -0.078125 to 0.078125
- queries: bfloat16 [8, 4096, 4096], P('section', 'dp'), may hold values from -100 to 100
- stashed_keys: bfloat16 [8, 4096, 512], P('section', 'dp'), may hold values from -5 to 5
- stashed_values: bfloat16 [8, 4096, 512], P('section', 'dp'), may hold values from -6 to 6
- out_cotangent: bfloat16 [8, 4096, 4096], P('section', 'dp'), may hold values from -6 to 6
- logprob_grad: bfloat16 [4096, 5120], P('dp'), may hold values from -2 to 2
- new_logprob: float32 [4096], P('dp'), may hold values from -5 to 0.5
- old_logprob: float32 [4096], P('dp'), may hold values from -5 to 0.5
- advantages: float32 [32, 4], P('dp'), may hold values from -3 to 3
- segment_ids: int32 [32, 128], P('dp'), may hold values from 0 to 3, never falling along the last dimension, each value on 1 to 96 neighbouring positions
Outputs:
- hidden_cotangent: bfloat16 [8, 4096, 5120], P('section', 'dp')
- key_weight_grad: float32 [8, 5120, 512], P('section', 'dp')
- value_weight_grad: float32 [8, 5120, 512], P('section', 'dp')
The draws below stay inside these ranges and needn't reach their ends.
Inputs may be any that keep to these rules, and one draw needn't show every extreme that they name: `segment_ids`: within each block the ids never fall, every rollout has 1 to 96 rows, and one has exactly 96.
All inputs are finite; a program needn't handle non-finite values.
Results may differ from the reference program's by a relative error of at most 0.023.
Values may be sent and summed in bfloat16 or wider, within the bound.
No kernel may reach another device: no remote copies, remote signals or barrier semaphores. Data moves between devices by JAX's collectives and lax.ppermute only.
A program may use at most 128 MiB of HBM per device.

```python
import math
import jax
import jax.numpy as jnp
import numpy as np
from jax import lax

D = 5120
HD = 128
KVH = 4
GROUP = 8
TOK_DEV = 128
SEGS = 4
QH = 32
KVW = 512
MOST = 96
SECTIONS = 8
BLOCKS = 32
TOKENS = 4096


def base_keys(key):
    return jnp.clip(jax.random.normal(key, (SECTIONS, TOKENS, KVW), jnp.float32), -5.0, 5.0)


def base_logprob(key):
    return jax.random.uniform(key, (TOKENS,), jnp.float32, -4.0, -0.5)


def draw_stashed_keys(key, part):
    base = base_keys(key)
    return base.astype(jnp.bfloat16)


def draw_queries(key, part):
    key = jax.random.fold_in(key, 12)
    fresh = jnp.clip(jax.random.normal(key, (SECTIONS, TOKENS, QH * HD), jnp.float32), -5.0, 5.0)
    return fresh.astype(jnp.bfloat16)


def draw_hidden_in(key, part):
    key = jax.random.fold_in(key, 13)
    noise_key, row_key, column_key = jax.random.split(key, 3)
    noise = jnp.clip(jax.random.normal(noise_key, (SECTIONS, TOKENS, D), jnp.float32), -4.0, 4.0)
    top_scale = 10.0
    row_scale = jnp.exp(jax.random.uniform(row_key, (SECTIONS, TOKENS, 1), jnp.float32) * math.log(top_scale))
    column_scale = jnp.exp(jax.random.uniform(column_key, (SECTIONS, 1, D), jnp.float32) * math.log(top_scale))
    return (noise * row_scale * column_scale).astype(jnp.bfloat16)


def draw_new_logprob(key, part):
    base = base_logprob(key)
    key = jax.random.fold_in(key, 14)
    offset = 0.25 * jnp.clip(jax.random.normal(key, (TOKENS,), jnp.float32), -4.0, 4.0)
    return base + offset


def draw_old_logprob(key, part):
    base = base_logprob(key)
    key = jax.random.fold_in(key, 15)
    offset = 0.25 * jnp.clip(jax.random.normal(key, (TOKENS,), jnp.float32), -4.0, 4.0)
    return base + offset


def level_of(own_key, extent, cuts, smallest, top_value):
    level, own = 1.0, jax.random.fold_in(own_key, 6)
    for dim, blocks in cuts:
        steps = jnp.exp(jax.random.uniform(jax.random.fold_in(own, dim), (blocks,), jnp.float32, smallest / len(cuts), top_value / len(cuts)))
        level = level * jnp.repeat(steps, extent[dim] // blocks).reshape([-1 if axis == dim else 1 for axis in range(len(extent))])
    return level


def length_profile(count, total, limit, lean):
    weights = [(1 << 20) // math.isqrt(grade ** lean) + 1 for grade in range(2, count + 1)]
    spare, counts = total - limit - (count - 1), [1] * (count - 1)
    while spare > 0:
        movable = [i for i in range(count - 1) if counts[i] < limit]
        whole, budget = sum([weights[i] for i in movable]), spare
        for i in movable:
            more = min(limit - counts[i], max(1, budget * weights[i] // whole), spare)
            counts[i] = counts[i] + more
            spare = spare - more
    return np.array([limit] + counts)


def ragged(stream_key, count, total, most, skew):
    if count == 2:
        one = jax.random.randint(stream_key, (), max(1, total - most), min(most, total - 1) + 1)
        return jnp.stack([one, total - one])
    lengths = jnp.asarray(length_profile(count, total, most, skew), jnp.int32)
    couples = (count - 1) // 2
    donor, sink = lengths[1:1 + 2 * couples:2], lengths[2:2 + 2 * couples:2]
    slack = jnp.minimum(donor - 1, most - sink)
    moved = jax.random.randint(jax.random.fold_in(stream_key, 1), (couples,), 0, 1 << 20) % (slack + 1)
    lengths = lengths.at[1:1 + 2 * couples:2].set(donor - moved).at[2:2 + 2 * couples:2].set(sink + moved)
    return lengths[jax.random.permutation(jax.random.fold_in(stream_key, 2), count)]


def scatter_about(key, extent, scale, most, pieces=(), held_as=jnp.bfloat16):
    values = jax.random.normal(key, extent, jnp.float32) * scale
    if len(pieces) > 0:
        values = level_of(key, extent, pieces, -0.22, 0.18) * values
    return jnp.clip(values, min=-most, max=most).astype(held_as)


def setup_inputs(seed: int = 0) -> dict:
    arg_keys = jax.random.split(jax.random.key(seed), 14)
    hidden_in = draw_hidden_in(jax.random.fold_in(arg_keys[13], 71), 0)
    norm_gain = jnp.clip(1.0 + 0.1 * jax.random.normal(arg_keys[1], (SECTIONS, D), jnp.float32), 0.5, 1.5).astype(jnp.bfloat16)
    key_weight = scatter_about(arg_keys[2], (SECTIONS, D, KVW), D ** -0.5, 0.078125, ((0, 8), (1, 32)))
    value_weight = scatter_about(arg_keys[3], (SECTIONS, D, KVW), D ** -0.5, 0.078125, ((0, 8), (1, 32)))
    queries = draw_queries(jax.random.fold_in(arg_keys[13], 71), 0)
    stashed_keys = draw_stashed_keys(jax.random.fold_in(arg_keys[13], 71), 0)
    stashed_values = scatter_about(arg_keys[6], (SECTIONS, TOKENS, KVW), 1.0, 6.0, ((0, 8), (1, 32)))
    out_cotangent = scatter_about(arg_keys[7], (SECTIONS, TOKENS, QH * HD), 1.0, 6.0, ((0, 8), (1, 32)))
    logprob_grad = scatter_about(arg_keys[8], (TOKENS, D), 0.3, 2.0, ((0, 32),))
    new_logprob = draw_new_logprob(jax.random.fold_in(arg_keys[13], 71), 0)
    old_logprob = draw_old_logprob(jax.random.fold_in(arg_keys[13], 71), 0)
    advantages = scatter_about(arg_keys[11], (BLOCKS, SEGS), 1.0, 3.0, ((0, 32),), jnp.float32)
    segment_ids = jax.vmap(lambda own: jnp.searchsorted(jnp.cumsum(ragged(own, SEGS, TOK_DEV, MOST, 2)), jnp.arange(TOK_DEV), side="right"))(jax.random.split(arg_keys[12], BLOCKS)).reshape((BLOCKS, TOK_DEV)).astype(jnp.int32)
    return dict(hidden_in=hidden_in, norm_gain=norm_gain, key_weight=key_weight, value_weight=value_weight, queries=queries, stashed_keys=stashed_keys, stashed_values=stashed_values, out_cotangent=out_cotangent, logprob_grad=logprob_grad, new_logprob=new_logprob, old_logprob=old_logprob, advantages=advantages, segment_ids=segment_ids)


EPSILON = 1e-06

def attend_back(queries, stashed_keys, stashed_values, out_cotangent, segments):
    row_count = queries.shape[0]
    score_scale = 1.0 / math.sqrt(HD)
    query_full = queries.reshape(row_count, KVH, GROUP, HD).astype(jnp.float32)
    key_full = stashed_keys.reshape(row_count, KVH, HD).astype(jnp.float32)
    value_full = stashed_values.reshape(row_count, KVH, HD).astype(jnp.float32)
    cot_full = out_cotangent.reshape(row_count, KVH, GROUP, HD).astype(jnp.float32)
    position = jnp.arange(row_count)
    allowed = (segments[:, None] == segments[None, :]) & (position[None, :] <= position[:, None])
    scores = jnp.einsum('igne,jge->gnij', query_full, key_full) * score_scale
    scores = jnp.where(allowed[None, None], scores, -jnp.inf)
    highest = lax.optimization_barrier(jnp.max(scores, axis=-1, keepdims=True))
    exp_scores = jnp.exp(scores - highest)
    probs_full = exp_scores / lax.optimization_barrier(jnp.sum(exp_scores, axis=-1, keepdims=True))
    probs_half = lax.optimization_barrier(probs_full.astype(jnp.bfloat16)).astype(jnp.float32)
    attended = jnp.einsum('gnij,jge->igne', probs_half, value_full)
    row_delta = lax.optimization_barrier(jnp.sum(cot_full * attended, axis=-1))
    prob_cot = jnp.einsum('igne,jge->gnij', cot_full, value_full)
    score_cot = probs_full * (prob_cot - jnp.transpose(row_delta, (1, 2, 0))[..., None])
    score_half = lax.optimization_barrier(score_cot.astype(jnp.bfloat16)).astype(jnp.float32)
    key_cot = jnp.einsum('gnij,igne->jge', score_half, query_full) * score_scale
    value_cot = jnp.einsum('gnij,igne->jge', probs_half, cot_full)
    return (key_cot.astype(jnp.bfloat16).reshape(row_count, KVW), value_cot.astype(jnp.bfloat16).reshape(row_count, KVW))

def add_block(running_sum, block_item):
    block_scaled, block_cot = block_item
    block_part = jnp.dot(block_scaled.T, block_cot, preferred_element_type=jnp.float32)
    block_part = lax.optimization_barrier(block_part.astype(jnp.bfloat16)).astype(jnp.float32)
    return (running_sum + block_part, None)

def reference(hidden_in, norm_gain, key_weight, value_weight, queries, stashed_keys, stashed_values, out_cotangent, logprob_grad, new_logprob, old_logprob, advantages, segment_ids):
    row_adv = jnp.take_along_axis(advantages, segment_ids, axis=1).reshape(TOKENS)
    ratio = jnp.exp(new_logprob - old_logprob)
    coefficient = -jnp.clip(ratio, 0.8, 1.28) * row_adv
    top_term = coefficient[:, None] * logprob_grad.astype(jnp.float32)
    running = jnp.zeros((TOKENS, D), jnp.float32)
    cotangents = []
    key_grads = []
    value_grads = []
    for section_index in range(SECTIONS - 1, -1, -1):
        stream = hidden_in[section_index].astype(jnp.float32)
        inv_rms = lax.rsqrt(lax.optimization_barrier(jnp.mean(stream * stream, axis=-1, keepdims=True)) + EPSILON)
        normed = stream * inv_rms
        gain_full = norm_gain[section_index].astype(jnp.float32)
        scaled = (normed * gain_full).astype(jnp.bfloat16)
        blocks = (queries[section_index].reshape(BLOCKS, TOK_DEV, QH * HD), stashed_keys[section_index].reshape(BLOCKS, TOK_DEV, KVW), stashed_values[section_index].reshape(BLOCKS, TOK_DEV, KVW), out_cotangent[section_index].reshape(BLOCKS, TOK_DEV, QH * HD), segment_ids)
        key_cot, value_cot = lax.map(lambda block_item: attend_back(*block_item), blocks)
        kv_cot = jnp.concatenate([key_cot, value_cot], axis=-1)
        weight_grad, unused = lax.scan(add_block, jnp.zeros((D, 2 * KVW), jnp.float32), (scaled.reshape(BLOCKS, TOK_DEV, D), kv_cot))
        key_grads.append(weight_grad[:, :KVW])
        value_grads.append(weight_grad[:, KVW:])
        weight_pair = jnp.concatenate([key_weight[section_index], value_weight[section_index]], axis=1)
        scaled_cot = jnp.dot(kv_cot.reshape(TOKENS, 2 * KVW), weight_pair.T, preferred_element_type=jnp.float32) * gain_full
        local_term = inv_rms * (scaled_cot - normed * lax.optimization_barrier(jnp.mean(scaled_cot * normed, axis=-1, keepdims=True)))
        running = running + local_term
        cotangents.append((top_term + running).astype(jnp.bfloat16))
    return (jnp.stack(cotangents[::-1]), jnp.stack(key_grads[::-1]), jnp.stack(value_grads[::-1]))
```

```python
import functools
import math

import jax
import jax.numpy as jnp
from jax import lax
from jax.experimental import pallas as pl
from jax.experimental.pallas import tpu as pltpu
from jax.sharding import PartitionSpec as P

D = 5120
HD = 128
KVH = 4
GROUP = 8
KVW = 512
ROWS = 128
NZ = 8
NX = 4
NY = 4
SLAB = D // (NZ * NX)
EPSILON = 1e-06
VMEM = pltpu.CompilerParams(vmem_limit_bytes=48 * 1024 * 1024)
NT = (((1,), (1,)), ((), ()))

Z_FIRST = (0, 1, 7, 2, 6)
Z_LAST = (3, 5, 4)


def shape_of(shape, dtype=jnp.bfloat16):
    return jax.ShapeDtypeStruct(shape, dtype)


def whole(count):
    return [pl.BlockSpec(memory_space=pltpu.VMEM)] * count


def fetched(*shapes):
    return [pl.BlockSpec(shape, lambda *_, n=len(shape): (0,) * n) for shape in shapes]


def after(values, *first):
    return lax.optimization_barrier((values, first))[0]


def cost(flops, moved, exps=0):
    return pl.CostEstimate(flops=flops, bytes_accessed=moved, transcendentals=exps)


def shift_z(value, step):
    pairs = [(z * NX + x, ((z + step) % NZ) * NX + x) for z in range(NZ) for x in range(NX)]
    return lax.ppermute(value, "dp", pairs)


def shift_x(value, step):
    pairs = [(z * NX + x, z * NX + (x + step) % NX) for z in range(NZ) for x in range(NX)]
    return lax.ppermute(value, "dp", pairs)


def swap_core(value):
    return lax.ppermute(value, "section", [(s, s ^ 1) for s in range(2 * NY)])


def send_y(value, routes):
    pairs = [(2 * a + c, 2 * b + c) for a, b in routes for c in range(2)]
    return lax.ppermute(value, "section", pairs)


def place():
    own = lax.axis_index("dp")
    layer = lax.axis_index("section")
    return own // NX, own % NX, layer // 2, layer % 2


def turn_kernel(h_ref, o0, o1, o2, o3, held):
    z, x, _, _ = place()
    for tile in range(D // 128):
        turned = h_ref[:, tile * 128 : (tile + 1) * 128].T
        for piece in range(4):
            unit = tile * 4 + piece
            slab, part = unit // 5, unit % 5
            k = lax.rem(slab // NX - z + NZ, NZ)
            d = lax.rem(slab % NX - x + NX, NX)
            held[d, k, part * 32 : (part + 1) * 32, :] = turned[piece * 32 : (piece + 1) * 32, :]
    for d, out in enumerate((o0, o1, o2, o3)):
        out[...] = held[d]


def turn(hidden):
    return pl.pallas_call(
        turn_kernel,
        out_shape=[shape_of((NZ, SLAB, ROWS))] * NX,
        in_specs=fetched((ROWS, D)),
        out_specs=whole(NX),
        scratch_shapes=[pltpu.VMEM((NX, NZ, SLAB, ROWS), jnp.bfloat16)],
        compiler_params=VMEM,
        cost_estimate=cost(0, 4 * D * ROWS),
        name="turn",
    )(hidden)


def attend_kernel(q_ref, k_ref, v_ref, o_ref, row_ref, h_ref, out_ref):
    squares = jnp.zeros((ROWS, 128), jnp.float32)
    for tile in range(D // 128):
        part = h_ref[:, tile * 128 : (tile + 1) * 128].astype(jnp.float32)
        squares = squares + part * part
    inv_rms = lax.rsqrt(jnp.sum(squares, axis=1, keepdims=True) * (1.0 / D) + EPSILON)
    j_place = lax.broadcasted_iota(jnp.int32, (ROWS, ROWS), 0)
    i_place = lax.broadcasted_iota(jnp.int32, (ROWS, ROWS), 1)
    segment = jnp.broadcast_to(row_ref[...].astype(jnp.float32), (ROWS, ROWS))
    allowed = (segment.T == segment) & (j_place <= i_place)
    scale = 1.0 / math.sqrt(HD)
    for g in range(KVH):
        key = k_ref[:, g * HD : (g + 1) * HD]
        value = v_ref[:, g * HD : (g + 1) * HD]
        heads = range(g * GROUP, (g + 1) * GROUP)
        query = jnp.concatenate([q_ref[:, n * HD : (n + 1) * HD] for n in heads], axis=0)
        cot = jnp.concatenate([o_ref[:, n * HD : (n + 1) * HD] for n in heads], axis=0)
        scores = lax.dot_general(key, query, NT, preferred_element_type=jnp.float32) * scale
        prob_cot = lax.dot_general(value, cot, NT, preferred_element_type=jnp.float32)
        halves, cots = [], []
        for n in range(GROUP):
            span = slice(n * ROWS, (n + 1) * ROWS)
            score = jnp.where(allowed, scores[:, span], -jnp.inf)
            high = jnp.max(score, axis=0, keepdims=True)
            grown = jnp.exp(score - high)
            probs = grown * (1.0 / jnp.sum(grown, axis=0, keepdims=True))
            half = probs.astype(jnp.bfloat16)
            pulled = prob_cot[:, span]
            delta = jnp.sum(half.astype(jnp.float32) * pulled, axis=0, keepdims=True)
            halves.append(half)
            cots.append((probs * (pulled - delta)).astype(jnp.bfloat16))
        key_cot = jnp.dot(jnp.concatenate(cots, axis=1), query, preferred_element_type=jnp.float32)
        value_cot = jnp.dot(jnp.concatenate(halves, axis=1), cot, preferred_element_type=jnp.float32)
        key_cot = (key_cot * scale).astype(jnp.bfloat16).astype(jnp.float32)
        value_cot = value_cot.astype(jnp.bfloat16).astype(jnp.float32)
        out_ref[:, g * HD : (g + 1) * HD] = (key_cot * inv_rms).astype(jnp.bfloat16)
        out_ref[:, KVW + g * HD : KVW + (g + 1) * HD] = (value_cot * inv_rms).astype(jnp.bfloat16)


def attend(queries, keys, values, cotangent, row, hidden):
    return pl.pallas_call(
        attend_kernel,
        out_shape=shape_of((ROWS, 2 * KVW)),
        in_specs=fetched(
            (ROWS, KVH * GROUP * HD), (ROWS, KVW), (ROWS, KVW), (ROWS, KVH * GROUP * HD), (1, ROWS), (ROWS, D)
        ),
        out_specs=pl.BlockSpec(memory_space=pltpu.VMEM),
        compiler_params=VMEM,
        cost_estimate=cost(4 * 32 * 2 * 128**3, 4 * 2**20, 32 * 128 * 128),
        name="attend",
    )(queries, keys, values, cotangent, row, hidden)


def grad_kernel(*refs):
    turned, cots, outs = refs[:NX], refs[NX : 2 * NX], refs[2 * NX : 2 * NX + NZ]
    left = jnp.concatenate([ref[...].reshape(NZ * SLAB, ROWS) for ref in turned], axis=1)
    right = jnp.concatenate([ref[...] for ref in cots], axis=0)
    for k in range(NZ):
        outs[k][...] = jnp.dot(
            left[k * SLAB : (k + 1) * SLAB], right, preferred_element_type=jnp.float32
        ).astype(jnp.bfloat16)


def weight_terms(turned, cots):
    return pl.pallas_call(
        grad_kernel,
        out_shape=[shape_of((SLAB, 2 * KVW))] * NZ,
        in_specs=whole(2 * NX),
        out_specs=whole(NZ),
        compiler_params=VMEM,
        cost_estimate=cost(2 * 512 * 1280 * 1024, 6 * 2**20),
        name="weight_terms",
    )(*turned, *cots)


def back_kernel(slabs, *refs):
    weights, cots, outs = refs[: len(slabs)], refs[len(slabs) : len(slabs) + NX], refs[len(slabs) + NX :]
    right = jnp.concatenate([ref[...] for ref in cots], axis=0)
    for place_k, weight in enumerate(weights):
        full = lax.dot_general(weight[...], right, NT, preferred_element_type=jnp.float32)
        for d in range(NX):
            outs[d][place_k] = full[:, d * ROWS : (d + 1) * ROWS].astype(jnp.bfloat16)


def back(weights, cots):
    count = len(weights)
    return pl.pallas_call(
        functools.partial(back_kernel, tuple(range(count))),
        out_shape=[shape_of((count, SLAB, ROWS))] * NX,
        in_specs=whole(count + NX),
        out_specs=whole(NX),
        compiler_params=VMEM,
        cost_estimate=cost(2 * 512 * 160 * count * 1024, 2**20 * 3),
        name="back",
    )(*weights, *cots)


def local_kernel(*refs):
    firsts, lasts, turned = refs[:NX], refs[NX : 2 * NX], refs[2 * NX : 3 * NX]
    mine, other = refs[3 * NX : 3 * NX + 2], refs[3 * NX + 2 : 3 * NX + 4]
    held = refs[3 * NX + 4]
    _, _, _, core = place()
    squares = jnp.zeros((SLAB, ROWS), jnp.float32)
    along = jnp.zeros((SLAB, ROWS), jnp.float32)
    order = [(firsts, place_k, k) for place_k, k in enumerate(Z_FIRST)]
    order += [(lasts, place_k, k) for place_k, k in enumerate(Z_LAST)]
    for d in range(NX):
        for source, place_k, k in order:
            stream = turned[d][k].astype(jnp.float32)
            squares = squares + stream * stream
            along = along + stream * source[d][place_k].astype(jnp.float32)
    inv_rms = lax.rsqrt(jnp.sum(squares, axis=0, keepdims=True) * (1.0 / D) + EPSILON)
    pull = inv_rms * inv_rms * (jnp.sum(along, axis=0, keepdims=True) * (1.0 / D))
    for d in range(NX):
        for source, place_k, k in order:
            stream = turned[d][k].astype(jnp.float32)
            term = source[d][place_k].astype(jnp.float32) - stream * pull
            held[k // 4, k % 4, d] = term.astype(jnp.bfloat16)
    for chunk in range(2):
        mine[chunk][...] = held[core, 2 * chunk : 2 * chunk + 2]
        other[chunk][...] = held[1 - core, 2 * chunk : 2 * chunk + 2]


def local_terms(firsts, lasts, turned):
    return pl.pallas_call(
        local_kernel,
        out_shape=[shape_of((2, NX, SLAB, ROWS))] * 4,
        in_specs=whole(3 * NX),
        out_specs=whole(4),
        scratch_shapes=[pltpu.VMEM((2, 4, NX, SLAB, ROWS), jnp.bfloat16)],
        compiler_params=VMEM,
        cost_estimate=cost(0, 4 * 2**20),
        name="local_terms",
    )(*firsts, *lasts, *turned)


FINISH_STEPS = 5
FINISH_WIDE = D // FINISH_STEPS


def finish_kernel(*refs):
    pieces, (top_ref, new_ref, old_ref, adv_ref, row_ref) = refs[:14], refs[14:19]
    out_ref, total, coef = refs[19:]
    z, x, _, core = place()
    below = (1 - core).astype(jnp.float32)
    step = pl.program_id(0)

    @pl.when(step == 0)
    def _():
        for chunk in range(2):
            mine, met, down, wrap, swap, other, back_in = pieces[chunk * 7 : chunk * 7 + 7]
            for a in range(2):
                for d in range(NX):
                    own = mine[a, d].astype(jnp.float32) + below * met[a, d].astype(jnp.float32)
                    upper = down[a, d].astype(jnp.float32) + wrap[a, d].astype(jnp.float32)
                    own = own + (upper + swap[a, d].astype(jnp.float32))
                    rest = other[a, d].astype(jnp.float32) + back_in[a, d].astype(jnp.float32)
                    column = lax.rem(x + d, NX)
                    for value, half in ((own, core), (rest, 1 - core)):
                        k = half * 4 + (2 * chunk + a)
                        slab = lax.rem(z + k, NZ) * NX + column
                        total[pl.ds(pl.multiple_of(slab * SLAB, 32), SLAB), :] = value
        rollout = row_ref[...]
        advantage = jnp.zeros((1, ROWS), jnp.float32)
        for index in range(4):
            advantage = advantage + jnp.where(rollout == index, adv_ref[0, index], 0.0)
        ratio = jnp.exp(new_ref[...] - old_ref[...])
        across = -jnp.clip(ratio, 0.8, 1.28) * advantage
        coef[...] = jnp.broadcast_to(across, (ROWS, ROWS)).T

    coefficient = coef[...]
    for tile in range(FINISH_WIDE // 128):
        span = slice(tile * 128, (tile + 1) * 128)
        first = pl.multiple_of(step * FINISH_WIDE + tile * 128, 128)
        turned = total[pl.ds(first, 128), :].T
        top = coefficient * top_ref[:, span].astype(jnp.float32)
        out_ref[:, span] = (top + turned).astype(jnp.bfloat16)


def finish(pieces, top, new_logprob, old_logprob, advantages, segments):
    return pl.pallas_call(
        finish_kernel,
        grid=(FINISH_STEPS,),
        out_shape=shape_of((ROWS, D)),
        in_specs=whole(14)
        + [pl.BlockSpec((ROWS, FINISH_WIDE), lambda step: (0, step))]
        + fetched((1, ROWS), (1, ROWS))
        + [pl.BlockSpec(memory_space=pltpu.SMEM)]
        + fetched((1, ROWS)),
        out_specs=pl.BlockSpec((ROWS, FINISH_WIDE), lambda step: (0, step)),
        scratch_shapes=[pltpu.VMEM((D, ROWS), jnp.float32), pltpu.VMEM((ROWS, ROWS), jnp.float32)],
        compiler_params=VMEM,
        cost_estimate=cost(0, 8 * 2**20),
        name="finish",
    )(*pieces, top, new_logprob, old_logprob, advantages, segments)


def scatter_z(terms):
    half = SLAB // 2
    wide = jnp.float32

    def add(first, second):
        return (first.astype(wide) + second.astype(wide)).astype(jnp.bfloat16)

    far_up, far_down = shift_z(terms[4][:half], 1), shift_z(terms[4][half:], -1)
    up = jnp.concatenate([add(terms[3][:half], far_up), terms[3][half:]], axis=0)
    down = jnp.concatenate([terms[5][:half], add(terms[5][half:], far_down)], axis=0)
    up, down = shift_z(up, 1), shift_z(down, -1)
    up, down = add(terms[2], up), add(terms[6], down)
    up, down = shift_z(up, 1), shift_z(down, -1)
    up, down = add(terms[1], up), add(terms[7], down)
    up, down = shift_z(up, 1), shift_z(down, -1)
    return terms[0].astype(wide) + (up.astype(wide) + down.astype(wide))


def local(
    hidden_in,
    norm_gain,
    key_weight,
    value_weight,
    queries,
    stashed_keys,
    stashed_values,
    out_cotangent,
    logprob_grad,
    new_logprob,
    old_logprob,
    advantages,
    segment_ids,
):
    wide = jnp.float32
    _, _, y, core = place()
    hidden = hidden_in[0]
    gain = norm_gain[0].astype(wide)[:, None]
    weight_pair = jnp.concatenate([key_weight[0], value_weight[0]], axis=1).astype(wide)
    own = (weight_pair * gain).astype(jnp.bfloat16)
    half = SLAB // 2
    up_1, down_1 = shift_z(own, 1), shift_z(own, -1)

    turned = turn(hidden)
    met_turned = [turned[0]] + [shift_x(turned[d], d) for d in (1, 2, 3)]
    cots = attend(
        queries[0],
        stashed_keys[0],
        stashed_values[0],
        out_cotangent[0],
        after(segment_ids, *turned),
        hidden,
    )
    up_1, down_1 = after((up_1, down_1), cots)
    cots = after(cots, up_1, down_1, *met_turned)
    up_2, down_2 = shift_z(up_1, 1), shift_z(down_1, -1)
    met_cots = [cots] + [shift_x(cots, d) for d in (1, 2, 3)]
    up_3, down_3 = shift_z(up_2, 1), shift_z(down_2, -1)
    met_cots = after(met_cots, up_2, down_2)
    firsts = back([own, down_1, up_1, down_2, up_2], met_cots)
    firsts = [firsts[0]] + [shift_x(firsts[d], -d) for d in (1, 2, 3)]
    up_4, down_4 = shift_z(up_3[:half], 1), shift_z(down_3[half:], -1)
    met_turned = after(met_turned, up_3, down_3)
    terms = weight_terms(met_turned, met_cots)
    opposite = jnp.concatenate([up_4, down_4], axis=0)
    lasts = back([down_3, up_3, opposite], met_cots)
    lasts = [lasts[0]] + [shift_x(lasts[d], -d) for d in (1, 2, 3)]
    weight_grad = gain * scatter_z(after(terms, up_4, down_4))

    mine_a, mine_b, other_a, other_b = local_terms(firsts, lasts, turned)
    pieces, gate = [], ()
    for mine, other in ((mine_a, other_a), (mine_b, other_b)):
        met = swap_core(other)
        pair = (mine.astype(wide) + met.astype(wide)).astype(jnp.bfloat16)
        pair = after(pair, *gate)
        down = send_y(pair, [(3, 2), (2, 1)])
        wrap = send_y(pair, [(3, 0)])
        gate = (down, wrap)
        onward = jnp.where(y == 0, wrap.astype(wide), pair.astype(wide) + down.astype(wide))
        swap = send_y(onward.astype(jnp.bfloat16), [(0, 1), (1, 0)])
        upper = down.astype(wide) + wrap.astype(wide) + swap.astype(wide)
        upper = upper + jnp.where(core == 1, mine.astype(wide), 0.0)
        back_in = swap_core(upper.astype(jnp.bfloat16))
        pieces += [mine, met, down, wrap, swap, other, back_in]

    hidden_cotangent = finish(
        pieces, logprob_grad, new_logprob[None], old_logprob[None], advantages, segment_ids
    )
    return (
        hidden_cotangent[None],
        weight_grad[:, :KVW][None],
        weight_grad[:, KVW:][None],
    )


def solution(mesh):
    return jax.shard_map(
        local,
        mesh=mesh,
        in_specs=(
            P("section", "dp", None),
            P("section", "dp"),
            P("section", "dp", None),
            P("section", "dp", None),
            P("section", "dp", None),
            P("section", "dp", None),
            P("section", "dp", None),
            P("section", "dp", None),
            P("dp", None),
            P("dp"),
            P("dp"),
            P("dp", None),
            P("dp", None),
        ),
        out_specs=(P("section", "dp", None), P("section", "dp", None), P("section", "dp", None)),
        check_vma=False,
    )
```

```python
import functools
import math

import jax
import jax.numpy as jnp
from jax import lax
from jax.experimental import pallas as pl
from jax.experimental.pallas import tpu as pltpu
from jax.sharding import PartitionSpec as P

D = 5120
HD = 128
KVH = 4
GROUP = 8
KVW = 512
ROWS = 128
NZ = 8
NX = 4
NY = 4
SLAB = D // (NZ * NX)
EPSILON = 1e-06
VMEM = pltpu.CompilerParams(vmem_limit_bytes=48 * 1024 * 1024)
MOST_VMEM = pltpu.CompilerParams(vmem_limit_bytes=57 * 1024 * 1024)
NT = (((1,), (1,)), ((), ()))

Z_ORDER = (0, 1, 7, 2, 6, 3, 5, 4)
COTS = 2 * KVW // 128
RELAY = NZ * SLAB
RELAYED = NZ // 2 * SLAB + COTS // 2 * ROWS
SENT = RELAY + RELAYED + COTS // 2 * ROWS


def shape_of(shape, dtype=jnp.bfloat16):
    return jax.ShapeDtypeStruct(shape, dtype)


def whole(count):
    return [pl.BlockSpec(memory_space=pltpu.VMEM)] * count


def after(values, *first):
    return lax.optimization_barrier((values, first))[0]


def cost(flops, moved, exps=0):
    return pl.CostEstimate(flops=flops, bytes_accessed=moved, transcendentals=exps)


def shift_z(value, step):
    pairs = [(z * NX + x, ((z + step) % NZ) * NX + x) for z in range(NZ) for x in range(NX)]
    return lax.ppermute(value, "dp", pairs)


def shift_x(value, step):
    pairs = [(z * NX + x, z * NX + (x + step) % NX) for z in range(NZ) for x in range(NX)]
    return lax.ppermute(value, "dp", pairs)


def swap_core(value):
    return lax.ppermute(value, "section", [(s, s ^ 1) for s in range(2 * NY)])


def send_y(value, routes):
    pairs = [(2 * a + c, 2 * b + c) for a, b in routes for c in range(2)]
    return lax.ppermute(value, "section", pairs)


def place():
    own = lax.axis_index("dp")
    layer = lax.axis_index("section")
    return own // NX, own % NX, layer // 2, layer % 2


def start_copies(sources, targets, sems):
    copies = [
        pltpu.make_async_copy(source, target, sems.at[index])
        for index, (source, target) in enumerate(zip(sources, targets))
    ]
    for copy in copies:
        copy.start()
    return copies


def attend_kernel(*refs):
    sources, (out_ref, near_ref, up_ref, down_ref) = refs[:6], refs[6:10]
    targets, held, sems = refs[10:16], refs[16], refs[17]
    copies = start_copies(sources, targets, sems)
    h_ref, row_ref, k_ref, v_ref, q_ref, o_ref = targets
    z, x, _, _ = place()
    copies[0].wait()
    squares = jnp.zeros((ROWS, 128), jnp.float32)
    for tile in range(D // 128):
        part = h_ref[:, tile * 128 : (tile + 1) * 128]
        turned = part.T
        part = part.astype(jnp.float32)
        squares = squares + part * part
        for piece in range(4):
            unit = tile * 4 + piece
            slab, fifth = unit // 5, unit % 5
            k = lax.rem(slab // NX - z + NZ, NZ)
            d = lax.rem(slab % NX - x + NX, NX)
            held[d, k, fifth * 32 : (fifth + 1) * 32, :] = turned[piece * 32 : (piece + 1) * 32, :]
    near_ref[...] = held[0]
    for ref, d, first in ((up_ref, 1, 0), (down_ref, 3, NZ // 2)):
        for k in range(NZ):
            ref[k * SLAB : (k + 1) * SLAB, :] = held[d, k]
        for k in range(NZ // 2):
            ref[RELAY + k * SLAB : RELAY + (k + 1) * SLAB, :] = held[2, first + k]
    inv_rms = lax.rsqrt(jnp.sum(squares, axis=1, keepdims=True) * (1.0 / D) + EPSILON)
    for copy in copies[1:]:
        copy.wait()
    j_place = lax.broadcasted_iota(jnp.int32, (ROWS, ROWS), 0)
    i_place = lax.broadcasted_iota(jnp.int32, (ROWS, ROWS), 1)
    segment = jnp.broadcast_to(row_ref[...].astype(jnp.float32), (ROWS, ROWS))
    allowed = (segment.T == segment) & (j_place <= i_place)
    scale = 1.0 / math.sqrt(HD)
    for g in range(KVH):
        key = k_ref[:, g * HD : (g + 1) * HD]
        value = v_ref[:, g * HD : (g + 1) * HD]
        heads = range(g * GROUP, (g + 1) * GROUP)
        query = jnp.concatenate([q_ref[:, n * HD : (n + 1) * HD] for n in heads], axis=0)
        cot = jnp.concatenate([o_ref[:, n * HD : (n + 1) * HD] for n in heads], axis=0)
        scores = lax.dot_general(key, query, NT, preferred_element_type=jnp.float32) * scale
        prob_cot = lax.dot_general(value, cot, NT, preferred_element_type=jnp.float32)
        halves, cots = [], []
        for n in range(GROUP):
            span = slice(n * ROWS, (n + 1) * ROWS)
            score = jnp.where(allowed, scores[:, span], -jnp.inf)
            high = jnp.max(score, axis=0, keepdims=True)
            grown = jnp.exp(score - high)
            probs = grown * (1.0 / jnp.sum(grown, axis=0, keepdims=True))
            half = probs.astype(jnp.bfloat16)
            pulled = prob_cot[:, span]
            delta = jnp.sum(half.astype(jnp.float32) * pulled, axis=0, keepdims=True)
            halves.append(half)
            cots.append((probs * (pulled - delta)).astype(jnp.bfloat16))
        key_cot = jnp.dot(jnp.concatenate(cots, axis=1), query, preferred_element_type=jnp.float32)
        value_cot = jnp.dot(jnp.concatenate(halves, axis=1), cot, preferred_element_type=jnp.float32)
        key_cot = (key_cot * scale).astype(jnp.bfloat16).astype(jnp.float32)
        value_cot = value_cot.astype(jnp.bfloat16).astype(jnp.float32)
        for index, value in ((g, key_cot), (KVH + g, value_cot)):
            scaled = (value * inv_rms).astype(jnp.bfloat16)
            out_ref[:, index * HD : (index + 1) * HD] = scaled
            for ref, turn in ((up_ref, 0), (down_ref, KVH)):
                first = SENT - COTS * ROWS + (index + turn) % COTS * ROWS
                ref[first : first + ROWS, :] = scaled


def attend(hidden, row, keys, values, queries, cotangent):
    operands = (hidden, row, keys, values, queries, cotangent)
    return pl.pallas_call(
        attend_kernel,
        out_shape=[
            shape_of((ROWS, 2 * KVW)),
            shape_of((NZ, SLAB, ROWS)),
            shape_of((SENT, ROWS)),
            shape_of((SENT, ROWS)),
        ],
        in_specs=[pl.BlockSpec(memory_space=pl.ANY)] * 6,
        out_specs=whole(4),
        scratch_shapes=[pltpu.VMEM(a.shape, a.dtype) for a in operands]
        + [pltpu.VMEM((NX, NZ, SLAB, ROWS), jnp.bfloat16), pltpu.SemaphoreType.DMA((6,))],
        compiler_params=MOST_VMEM,
        cost_estimate=cost(4 * 32 * 2 * 128**3, 4 * 2**20, 32 * 128 * 128),
        name="attend",
    )(*operands)


def join_cots(cots, up, down, far_up, far_down, right):
    right[:ROWS] = cots[...]
    lead, far = SENT - COTS * ROWS, RELAYED - COTS // 2 * ROWS
    for tile in range(COTS):
        span = slice(tile * 128, (tile + 1) * 128)
        first = lead + tile * ROWS
        right[ROWS : 2 * ROWS, span] = up[first : first + ROWS]
        source, first = (far_up, far + tile * ROWS) if tile < COTS // 2 else (far_down, far + (tile - COTS // 2) * ROWS)
        right[2 * ROWS : 3 * ROWS, span] = source[first : first + ROWS]
        first = lead + (tile + COTS // 2) % COTS * ROWS
        right[3 * ROWS :, span] = down[first : first + ROWS]


def grad_kernel(near, cots, up, down, far_up, far_down, *refs):
    outs, left, right = refs[:NZ], refs[NZ], refs[NZ + 1]
    join_cots(cots, up, down, far_up, far_down, right)
    middle = NZ // 2 * SLAB
    left[:, :ROWS] = near[...].reshape(NZ * SLAB, ROWS)
    left[:, ROWS : 2 * ROWS] = up[: NZ * SLAB]
    left[:middle, 2 * ROWS : 3 * ROWS] = far_up[:middle]
    left[middle:, 2 * ROWS : 3 * ROWS] = far_down[:middle]
    left[:, 3 * ROWS :] = down[: NZ * SLAB]
    for k in range(NZ):
        outs[k][...] = jnp.dot(
            left[k * SLAB : (k + 1) * SLAB], right[...], preferred_element_type=jnp.float32
        ).astype(jnp.bfloat16)


def weight_terms(near, met):
    return pl.pallas_call(
        grad_kernel,
        out_shape=[shape_of((SLAB, 2 * KVW))] * NZ,
        in_specs=whole(6),
        out_specs=whole(NZ),
        scratch_shapes=[
            pltpu.VMEM((NZ * SLAB, NX * ROWS), jnp.bfloat16),
            pltpu.VMEM((NX * ROWS, 2 * KVW), jnp.bfloat16),
        ],
        compiler_params=VMEM,
        cost_estimate=cost(2 * 512 * 1280 * 1024, 6 * 2**20),
        name="weight_terms",
    )(near, *met)


def back_kernel(count, past, *refs):
    weights, cots = refs[:count], refs[count : count + 5]
    earlier, outs, right = refs[count + 5 : -1 - NX], refs[-1 - NX : -1], refs[-1]
    join_cots(*cots, right)
    for d, ref in enumerate(earlier):
        outs[d][:past] = ref[...]
    for place_k, weight in enumerate(weights, past):
        full = lax.dot_general(weight[...], right[...], NT, preferred_element_type=jnp.float32)
        for d in range(NX):
            outs[d][place_k] = full[:, d * ROWS : (d + 1) * ROWS].astype(jnp.bfloat16)


def back(weights, cots, earlier=()):
    count = len(weights)
    past = earlier[0].shape[0] if earlier else 0
    return pl.pallas_call(
        functools.partial(back_kernel, count, past),
        out_shape=[shape_of((past + count, SLAB, ROWS))] * NX,
        in_specs=whole(count + 5 + len(earlier)),
        out_specs=whole(NX),
        scratch_shapes=[pltpu.VMEM((NX * ROWS, 2 * KVW), jnp.bfloat16)],
        compiler_params=VMEM,
        cost_estimate=cost(2 * 512 * 160 * count * 1024, 2**20 * 3),
        name="back",
    )(*weights, *cots, *earlier)


def local_kernel(*refs):
    products, (near, up, down) = refs[:NX], refs[NX : NX + 3]
    mine, other, held = refs[NX + 3 : NX + 5], refs[NX + 5 : NX + 7], refs[-1]

    def stream_of(d, k):
        if d == 0:
            part = near[k]
        else:
            source = (None, up, up if k < NZ // 2 else down, down)[d]
            first = RELAY + k % (NZ // 2) * SLAB if d == 2 else k * SLAB
            part = source[first : first + SLAB, :]
        return part.astype(jnp.float32)

    _, _, _, core = place()
    squares = jnp.zeros((SLAB, ROWS), jnp.float32)
    along = jnp.zeros((SLAB, ROWS), jnp.float32)
    for d in range(NX):
        for place_k, k in enumerate(Z_ORDER):
            stream = stream_of(d, k)
            squares = squares + stream * stream
            along = along + stream * products[d][place_k].astype(jnp.float32)
    inv_rms = lax.rsqrt(jnp.sum(squares, axis=0, keepdims=True) * (1.0 / D) + EPSILON)
    pull = inv_rms * inv_rms * (jnp.sum(along, axis=0, keepdims=True) * (1.0 / D))
    for d in range(NX):
        for place_k, k in enumerate(Z_ORDER):
            stream = stream_of(d, k)
            term = products[d][place_k].astype(jnp.float32) - stream * pull
            held[k // 4, k % 4, d] = term.astype(jnp.bfloat16)
    for chunk in range(2):
        mine[chunk][...] = held[core, 2 * chunk : 2 * chunk + 2]
        other[chunk][...] = held[1 - core, 2 * chunk : 2 * chunk + 2]


def local_terms(products, turned):
    return pl.pallas_call(
        local_kernel,
        out_shape=[shape_of((2, NX, SLAB, ROWS))] * 4,
        in_specs=whole(NX + 3),
        out_specs=whole(4),
        scratch_shapes=[pltpu.VMEM((2, 4, NX, SLAB, ROWS), jnp.bfloat16)],
        compiler_params=VMEM,
        cost_estimate=cost(0, 4 * 2**20),
        name="local_terms",
    )(*products, *turned)


FINISH_STEPS = 5
FINISH_WIDE = D // FINISH_STEPS


def spread(total, half, value_of):
    z, x, _, _ = place()
    for a in range(4):
        for d in range(NX):
            slab = lax.rem(z + half * 4 + a, NZ) * NX + lax.rem(x + d, NX)
            total[pl.ds(pl.multiple_of(slab * SLAB, 32), SLAB), :] = value_of(a, d)


def part_of(chunks, a, d):
    return chunks[a // 2][a % 2, d].astype(jnp.float32)


def base_kernel(*refs):
    mine, met, other = refs[:2], refs[2:4], refs[4:6]
    top_ref, row_ref, out_ref, total, coef = refs[6:]
    _, _, _, core = place()
    below = (1 - core).astype(jnp.float32)
    step = pl.program_id(0)

    def own_of(a, d):
        return part_of(mine, a, d) + below * part_of(met, a, d)

    @pl.when(step == 0)
    def _():
        spread(total, core, own_of)
        spread(total, 1 - core, functools.partial(part_of, other))
        coef[...] = jnp.broadcast_to(row_ref[...], (ROWS, ROWS)).T

    coefficient = coef[...]
    for tile in range(FINISH_WIDE // 128):
        span = slice(tile * 128, (tile + 1) * 128)
        first = pl.multiple_of(step * FINISH_WIDE + tile * 128, 128)
        top = coefficient * top_ref[:, span].astype(jnp.float32)
        out_ref[:, span] = top + total[pl.ds(first, 128), :].T


def base_terms(mine, met, other, top, coefficient):
    return pl.pallas_call(
        base_kernel,
        grid=(FINISH_STEPS,),
        out_shape=shape_of((ROWS, D), jnp.float32),
        in_specs=whole(6) + [pl.BlockSpec((ROWS, FINISH_WIDE), lambda step: (0, step))] + whole(1),
        out_specs=pl.BlockSpec((ROWS, FINISH_WIDE), lambda step: (0, step)),
        scratch_shapes=[pltpu.VMEM((D, ROWS), jnp.float32), pltpu.VMEM((ROWS, ROWS), jnp.float32)],
        compiler_params=VMEM,
        cost_estimate=cost(0, 8 * 2**20),
        name="base_terms",
    )(*mine, *met, *other, top, coefficient)


def finish_kernel(*refs):
    wrap, down, swap, back_in = refs[:2], refs[2:4], refs[4:6], refs[6:8]
    base_ref, out_ref, total = refs[8:]
    _, _, _, core = place()
    step = pl.program_id(0)

    def upper_of(a, d):
        return part_of(wrap, a, d) + (part_of(down, a, d) + part_of(swap, a, d))

    @pl.when(step == 0)
    def _():
        spread(total, core, upper_of)
        spread(total, 1 - core, functools.partial(part_of, back_in))

    for tile in range(FINISH_WIDE // 128):
        span = slice(tile * 128, (tile + 1) * 128)
        first = pl.multiple_of(step * FINISH_WIDE + tile * 128, 128)
        out_ref[:, span] = (base_ref[:, span] + total[pl.ds(first, 128), :].T).astype(jnp.bfloat16)


def finish(wrap, down, swap, back_in, base):
    return pl.pallas_call(
        finish_kernel,
        grid=(FINISH_STEPS,),
        out_shape=shape_of((ROWS, D)),
        in_specs=whole(8) + [pl.BlockSpec((ROWS, FINISH_WIDE), lambda step: (0, step))],
        out_specs=pl.BlockSpec((ROWS, FINISH_WIDE), lambda step: (0, step)),
        scratch_shapes=[pltpu.VMEM((D, ROWS), jnp.float32)],
        compiler_params=VMEM,
        cost_estimate=cost(0, 6 * 2**20),
        name="finish",
    )(*wrap, *down, *swap, *back_in, base)


def scatter_z(terms):
    half = SLAB // 2
    wide = jnp.float32

    def add(first, second):
        return (first.astype(wide) + second.astype(wide)).astype(jnp.bfloat16)

    far_up, far_down = shift_z(terms[4][:half], 1), shift_z(terms[4][half:], -1)
    up = jnp.concatenate([add(terms[3][:half], far_up), terms[3][half:]], axis=0)
    down = jnp.concatenate([terms[5][:half], add(terms[5][half:], far_down)], axis=0)
    up, down = shift_z(up, 1), shift_z(down, -1)
    up, down = add(terms[2], up), add(terms[6], down)
    up, down = shift_z(up, 1), shift_z(down, -1)
    up, down = add(terms[1], up), add(terms[7], down)
    return terms[0], shift_z(up, 1), shift_z(down, -1)


def local(
    hidden_in,
    norm_gain,
    key_weight,
    value_weight,
    queries,
    stashed_keys,
    stashed_values,
    out_cotangent,
    logprob_grad,
    new_logprob,
    old_logprob,
    advantages,
    segment_ids,
):
    wide = jnp.float32
    _, _, y, core = place()
    half = SLAB // 2
    gain = norm_gain[0].astype(wide)[:, None]
    weight_pair = jnp.concatenate([key_weight[0], value_weight[0]], axis=1).astype(wide)
    own = (weight_pair * gain).astype(jnp.bfloat16)
    up_1, down_1 = shift_z(own, 1), shift_z(own, -1)

    cots, near, part_up, part_down = attend(
        hidden_in[0],
        after(segment_ids, own),
        stashed_keys[0],
        stashed_values[0],
        queries[0],
        out_cotangent[0],
    )
    up_1, down_1 = after((up_1, down_1), cots)
    met_up, met_down = shift_x(part_up, 1), shift_x(part_down, -1)
    up_2, down_2 = shift_z(up_1, 1), shift_z(down_1, -1)

    segments = after(segment_ids, up_1)[0]
    row_adv = jnp.zeros((ROWS,), wide)
    for index in range(advantages.shape[1]):
        row_adv = row_adv + jnp.where(segments == index, advantages[0, index], 0.0)
    ratio = jnp.exp(after(new_logprob, up_1) - old_logprob)
    coefficient = -jnp.clip(ratio, 0.8, 1.28) * row_adv
    up_2, down_2 = after((up_2, down_2), coefficient)

    up_3, down_3 = shift_z(up_2, 1), shift_z(down_2, -1)
    relay = slice(RELAY, RELAY + RELAYED)
    far_up, far_down = shift_x(met_up[relay], 1), shift_x(met_down[relay], -1)
    met = [cots, met_up, met_down, far_up, far_down]
    up_4, down_4 = shift_z(up_3[:half], 1), shift_z(down_3[half:], -1)

    firsts = back([own, down_1, up_1, down_2, up_2, down_3, up_3], met)
    opposite = jnp.concatenate([up_4, down_4], axis=0)
    products = back([opposite], met, firsts)
    met_late = after(met, products[0])
    products = [products[0]] + [shift_x(products[d], -d) for d in (1, 2, 3)]
    terms = weight_terms(near, met_late)
    sums = scatter_z(after(terms, products[1]))
    key_grad, value_grad = (
        gain * (sums[0][:, span].astype(wide) + (sums[1][:, span].astype(wide) + sums[2][:, span].astype(wide)))
        for span in (slice(0, KVW), slice(KVW, 2 * KVW))
    )

    *mine, other_a, other_b = local_terms(products, (near, part_up, part_down))
    other = [other_a, other_b]
    met_other = [swap_core(part) for part in other]
    pairs = [(own.astype(wide) + part.astype(wide)).astype(jnp.bfloat16) for own, part in zip(mine, met_other)]
    base = base_terms(mine, met_other, other, logprob_grad, after(coefficient[None], *pairs))
    wrap, down, swap, back_in = [], [], [], []
    for own, pair in zip(mine, pairs):
        wrap.append(send_y(pair, [(3, 0)]))
        down.append(send_y(pair, [(3, 2), (2, 1)]))
        if len(wrap) == 2:
            wrap[-1] = after(wrap[-1], base)
        onward = jnp.where(y == 0, wrap[-1].astype(wide), pair.astype(wide) + down[-1].astype(wide))
        swap.append(send_y(onward.astype(jnp.bfloat16), [(0, 1), (1, 0)]))
        upper = wrap[-1].astype(wide) + (down[-1].astype(wide) + swap[-1].astype(wide))
        upper = upper + jnp.where(core == 1, own.astype(wide), 0.0)
        back_in.append(swap_core(upper.astype(jnp.bfloat16)))
    hidden_cotangent = finish(wrap, down, swap, back_in, base)
    return hidden_cotangent[None], key_grad[None], value_grad[None]


def solution(mesh):
    return jax.shard_map(
        local,
        mesh=mesh,
        in_specs=(
            P("section", "dp", None),
            P("section", "dp"),
            P("section", "dp", None),
            P("section", "dp", None),
            P("section", "dp", None),
            P("section", "dp", None),
            P("section", "dp", None),
            P("section", "dp", None),
            P("dp", None),
            P("dp"),
            P("dp"),
            P("dp", None),
            P("dp", None),
        ),
        out_specs=(P("section", "dp", None), P("section", "dp", None), P("section", "dp", None)),
        check_vma=False,
    )
```

```python
import functools
import math

import jax
import jax.numpy as jnp
from jax import lax
from jax.experimental import pallas as pl
from jax.experimental.pallas import tpu as pltpu
from jax.sharding import PartitionSpec as P

D = 5120
HD = 128
KVH = 4
GROUP = 8
KVW = 512
ROWS = 128
NZ = 8
NX = 4
NY = 4
SLAB = D // (NZ * NX)
EPSILON = 1e-06
VMEM = pltpu.CompilerParams(vmem_limit_bytes=16 * 1024 * 1024)
MOST_VMEM = pltpu.CompilerParams(vmem_limit_bytes=57 * 1024 * 1024)
NT = (((1,), (1,)), ((), ()))

Z_ORDER = (0, 1, 7, 2, 6, 3, 5, 4)
HALVED = (3, 4, 5)
TERM_ROWS = [SLAB] * 3 + [SLAB // 2] * 6 + [SLAB] * 2
COTS = 2 * KVW // 128
STREAM = NZ * SLAB
RELAY = STREAM
RELAYED = NZ // 2 * SLAB + COTS // 2 * ROWS
SENT = RELAY + RELAYED + COTS // 2 * ROWS


def shape_of(shape, dtype=jnp.bfloat16):
    return jax.ShapeDtypeStruct(shape, dtype)


def whole(count):
    return [pl.BlockSpec(memory_space=pltpu.VMEM)] * count


def after(values, *first):
    return lax.optimization_barrier((values, first))[0]


def cost(flops, moved, exps=0):
    return pl.CostEstimate(flops=flops, bytes_accessed=moved, transcendentals=exps)


def shift_z(value, step):
    pairs = [(z * NX + x, ((z + step) % NZ) * NX + x) for z in range(NZ) for x in range(NX)]
    return lax.ppermute(value, "dp", pairs)


def shift_x(value, step):
    pairs = [(z * NX + x, z * NX + (x + step) % NX) for z in range(NZ) for x in range(NX)]
    return lax.ppermute(value, "dp", pairs)


def swap_core(value):
    return lax.ppermute(value, "section", [(s, s ^ 1) for s in range(2 * NY)])


def send_y(value, routes):
    pairs = [(2 * a + c, 2 * b + c) for a, b in routes for c in range(2)]
    return lax.ppermute(value, "section", pairs)


def place():
    own = lax.axis_index("dp")
    layer = lax.axis_index("section")
    return own // NX, own % NX, layer // 2, layer % 2


def start_copies(sources, targets, sems):
    copies = [
        pltpu.make_async_copy(source, target, sems.at[index])
        for index, (source, target) in enumerate(zip(sources, targets))
    ]
    for copy in copies:
        copy.start()
    return copies


def attend_kernel(*refs):
    (h_hbm, row_hbm, k_hbm, v_hbm, q_hbm, o_hbm), (cots_out, near_out, up_out, down_out) = refs[:6], refs[6:10]
    h_ref, row_ref, k_ref, v_ref, q_ref, o_ref, held, tiles, in_sems, out_sems = refs[10:]
    pieces = [
        (hbm.at[:, first : first + wide], ref.at[:, first : first + wide])
        for hbm, ref, wide in ((h_hbm, h_ref, D // 4),)
        for first in range(0, D, wide)
    ]
    pieces += [(row_hbm, row_ref), (k_hbm, k_ref), (v_hbm, v_ref)]
    for g in range(KVH):
        span = slice(g * GROUP * HD, (g + 1) * GROUP * HD)
        pieces += [(q_hbm.at[:, span], q_ref.at[:, span]), (o_hbm.at[:, span], o_ref.at[:, span])]
    copies = start_copies([pair[0] for pair in pieces], [pair[1] for pair in pieces], in_sems)
    z, x, _, _ = place()
    squares = jnp.zeros((ROWS, 128), jnp.float32)
    for tile in range(D // 128):
        if tile % 10 == 0:
            copies[tile // 10].wait()
        part = h_ref[:, tile * 128 : (tile + 1) * 128]
        turned = part.T
        part = part.astype(jnp.float32)
        squares = squares + part * part
        for piece in range(4):
            unit = tile * 4 + piece
            slab, fifth = unit // 5, unit % 5
            k = lax.rem(slab // NX - z + NZ, NZ)
            d = lax.rem(slab % NX - x + NX, NX)
            first = pl.multiple_of(k * SLAB + fifth * 32, 32)
            held[d, pl.ds(first, 32), :] = turned[piece * 32 : (piece + 1) * 32, :]
    middle = STREAM // 2
    sent = start_copies(
        [held.at[0], held.at[1], held.at[2, :middle], held.at[3], held.at[2, middle:]],
        [
            near_out,
            up_out.at[:STREAM],
            up_out.at[STREAM : STREAM + middle],
            down_out.at[:STREAM],
            down_out.at[STREAM : STREAM + middle],
        ],
        out_sems,
    )
    inv_rms = lax.rsqrt(jnp.sum(squares, axis=1, keepdims=True) * (1.0 / D) + EPSILON)
    for copy in copies[4:7]:
        copy.wait()
    j_place = lax.broadcasted_iota(jnp.int32, (ROWS, ROWS), 0)
    i_place = lax.broadcasted_iota(jnp.int32, (ROWS, ROWS), 1)
    segment = jnp.broadcast_to(row_ref[...].astype(jnp.float32), (ROWS, ROWS))
    allowed = (segment.T == segment) & (j_place <= i_place)
    scale = 1.0 / math.sqrt(HD)
    for g in range(KVH):
        for copy in copies[7 + 2 * g : 9 + 2 * g]:
            copy.wait()
        key = k_ref[:, g * HD : (g + 1) * HD]
        value = v_ref[:, g * HD : (g + 1) * HD]
        heads = range(g * GROUP, (g + 1) * GROUP)
        query = jnp.concatenate([q_ref[:, n * HD : (n + 1) * HD] for n in heads], axis=0)
        cot = jnp.concatenate([o_ref[:, n * HD : (n + 1) * HD] for n in heads], axis=0)
        scores = lax.dot_general(key, query, NT, preferred_element_type=jnp.float32) * scale
        prob_cot = lax.dot_general(value, cot, NT, preferred_element_type=jnp.float32)
        halves, cots = [], []
        for n in range(GROUP):
            span = slice(n * ROWS, (n + 1) * ROWS)
            score = jnp.where(allowed, scores[:, span], -jnp.inf)
            high = jnp.max(score, axis=0, keepdims=True)
            grown = jnp.exp(score - high)
            probs = grown * (1.0 / jnp.sum(grown, axis=0, keepdims=True))
            half = probs.astype(jnp.bfloat16)
            pulled = prob_cot[:, span]
            delta = jnp.sum(half.astype(jnp.float32) * pulled, axis=0, keepdims=True)
            halves.append(half)
            cots.append((probs * (pulled - delta)).astype(jnp.bfloat16))
        key_cot = jnp.dot(jnp.concatenate(cots, axis=1), query, preferred_element_type=jnp.float32)
        value_cot = jnp.dot(jnp.concatenate(halves, axis=1), cot, preferred_element_type=jnp.float32)
        key_cot = (key_cot * scale).astype(jnp.bfloat16).astype(jnp.float32)
        value_cot = value_cot.astype(jnp.bfloat16).astype(jnp.float32)
        for index, value in ((g, key_cot), (KVH + g, value_cot)):
            tiles[index * ROWS : (index + 1) * ROWS, :] = (value * inv_rms).astype(jnp.bfloat16)
    part, lead = COTS // 2 * ROWS, STREAM + STREAM // 2
    sent += start_copies(
        [tiles, tiles, tiles.at[part:], tiles.at[:part]],
        [cots_out, up_out.at[lead:], down_out.at[lead : lead + part], down_out.at[lead + part :]],
        out_sems.at[5:],
    )
    for copy in sent:
        copy.wait()


def attend(hidden, row, keys, values, queries, cotangent):
    operands = (hidden, row, keys, values, queries, cotangent)
    return pl.pallas_call(
        attend_kernel,
        out_shape=[shape_of((COTS * ROWS, ROWS)), shape_of((STREAM, ROWS)), shape_of((SENT, ROWS)), shape_of((SENT, ROWS))],
        in_specs=[pl.BlockSpec(memory_space=pl.ANY)] * 6,
        out_specs=[pl.BlockSpec(memory_space=pl.ANY)] * 4,
        scratch_shapes=[pltpu.VMEM(a.shape, a.dtype) for a in operands]
        + [
            pltpu.VMEM((NX, STREAM, ROWS), jnp.bfloat16),
            pltpu.VMEM((COTS * ROWS, ROWS), jnp.bfloat16),
            pltpu.SemaphoreType.DMA((15,)),
            pltpu.SemaphoreType.DMA((9,)),
        ],
        compiler_params=MOST_VMEM,
        cost_estimate=cost(4 * 32 * 2 * 128**3, 4 * 2**20, 32 * 128 * 128),
        name="attend",
    )(*operands)


def join_cots(cots, up, down, far_up, far_down, right):
    lead, far = SENT - COTS * ROWS, RELAYED - COTS // 2 * ROWS
    for tile in range(COTS):
        span = slice(tile * 128, (tile + 1) * 128)
        right[:ROWS, span] = cots[tile * ROWS : (tile + 1) * ROWS]
        first = lead + tile * ROWS
        right[ROWS : 2 * ROWS, span] = up[first : first + ROWS]
        source, first = (far_up, far + tile * ROWS) if tile < COTS // 2 else (far_down, far + (tile - COTS // 2) * ROWS)
        right[2 * ROWS : 3 * ROWS, span] = source[first : first + ROWS]
        first = lead + (tile + COTS // 2) % COTS * ROWS
        right[3 * ROWS :, span] = down[first : first + ROWS]


def grad_kernel(near, cots, up, down, far_up, far_down, *refs):
    outs, (left, right) = refs[:-2], refs[-2:]
    join_cots(cots, up, down, far_up, far_down, right)
    middle = NZ // 2 * SLAB
    left[:, :ROWS] = near[...]
    left[:, ROWS : 2 * ROWS] = up[: NZ * SLAB]
    left[:middle, 2 * ROWS : 3 * ROWS] = far_up[:middle]
    left[middle:, 2 * ROWS : 3 * ROWS] = far_down[:middle]
    left[:, 3 * ROWS :] = down[: NZ * SLAB]
    place_k, half = 0, SLAB // 2
    for k in range(NZ):
        term = jnp.dot(
            left[k * SLAB : (k + 1) * SLAB], right[...], preferred_element_type=jnp.float32
        ).astype(jnp.bfloat16)
        if k in HALVED:
            outs[place_k][...] = term[:half]
            outs[place_k + 1][...] = term[half:]
        else:
            outs[place_k][...] = term
        place_k += 2 if k in HALVED else 1


def weight_terms(near, met):
    return pl.pallas_call(
        grad_kernel,
        out_shape=[shape_of((rows, 2 * KVW)) for rows in TERM_ROWS],
        in_specs=whole(6),
        out_specs=whole(len(TERM_ROWS)),
        scratch_shapes=[
            pltpu.VMEM((NZ * SLAB, NX * ROWS), jnp.bfloat16),
            pltpu.VMEM((NX * ROWS, 2 * KVW), jnp.bfloat16),
        ],
        compiler_params=VMEM,
        cost_estimate=cost(2 * 512 * 1280 * 1024, 6 * 2**20),
        name="weight_terms",
    )(near, *met)


def back_kernel(*refs):
    weights, cots, outs, right = refs[:NZ], refs[NZ : NZ + 5], refs[NZ + 5 : -1], refs[-1]
    join_cots(*cots, right)
    for place_k, weight in enumerate(weights):
        full = lax.dot_general(weight[...], right[...], NT, preferred_element_type=jnp.float32)
        for d in range(NX):
            outs[d][place_k] = full[:, d * ROWS : (d + 1) * ROWS].astype(jnp.bfloat16)


def back(weights, cots):
    return pl.pallas_call(
        back_kernel,
        out_shape=[shape_of((NZ, SLAB, ROWS))] * NX,
        in_specs=whole(NZ + 5),
        out_specs=whole(NX),
        scratch_shapes=[pltpu.VMEM((NX * ROWS, 2 * KVW), jnp.bfloat16)],
        compiler_params=VMEM,
        cost_estimate=cost(2 * 512 * 1280 * 1024, 2**20 * 5),
        name="back",
    )(*weights, *cots)


def local_kernel(*refs):
    products, (near, up, down) = refs[:NX], refs[NX : NX + 3]
    mine, other, held = refs[NX + 3 : NX + 5], refs[NX + 5 : NX + 7], refs[-1]

    def stream_of(d, k):
        if d == 0:
            part = near[k * SLAB : (k + 1) * SLAB]
        else:
            source = (None, up, up if k < NZ // 2 else down, down)[d]
            first = RELAY + k % (NZ // 2) * SLAB if d == 2 else k * SLAB
            part = source[first : first + SLAB, :]
        return part.astype(jnp.float32)

    _, _, _, core = place()
    squares = jnp.zeros((SLAB, ROWS), jnp.float32)
    along = jnp.zeros((SLAB, ROWS), jnp.float32)
    for d in range(NX):
        for place_k, k in enumerate(Z_ORDER):
            stream = stream_of(d, k)
            squares = squares + stream * stream
            along = along + stream * products[d][place_k].astype(jnp.float32)
    inv_rms = lax.rsqrt(jnp.sum(squares, axis=0, keepdims=True) * (1.0 / D) + EPSILON)
    pull = inv_rms * inv_rms * (jnp.sum(along, axis=0, keepdims=True) * (1.0 / D))
    for d in range(NX):
        for place_k, k in enumerate(Z_ORDER):
            stream = stream_of(d, k)
            term = products[d][place_k].astype(jnp.float32) - stream * pull
            held[k // 4, k % 4, d] = term.astype(jnp.bfloat16)
    for chunk in range(2):
        mine[chunk][...] = held[core, 2 * chunk : 2 * chunk + 2]
        other[chunk][...] = held[1 - core, 2 * chunk : 2 * chunk + 2]


def local_terms(products, turned):
    return pl.pallas_call(
        local_kernel,
        out_shape=[shape_of((2, NX, SLAB, ROWS))] * 4,
        in_specs=whole(NX + 3),
        out_specs=whole(4),
        scratch_shapes=[pltpu.VMEM((2, 4, NX, SLAB, ROWS), jnp.bfloat16)],
        compiler_params=VMEM,
        cost_estimate=cost(0, 4 * 2**20),
        name="local_terms",
    )(*products, *turned)


FINISH_STEPS = 5
FINISH_WIDE = D // FINISH_STEPS


def spread(total, half, value_of):
    z, x, _, _ = place()
    for a in range(4):
        for d in range(NX):
            slab = lax.rem(z + half * 4 + a, NZ) * NX + lax.rem(x + d, NX)
            total[pl.ds(pl.multiple_of(slab * SLAB, 32), SLAB), :] = value_of(a, d)


def part_of(chunks, a, d):
    return chunks[a // 2][a % 2, d].astype(jnp.float32)


def base_kernel(*refs):
    mine, met, other = refs[:2], refs[2:4], refs[4:6]
    top_ref, row_ref, out_ref, total, coef = refs[6:]
    _, _, _, core = place()
    below = (1 - core).astype(jnp.float32)
    step = pl.program_id(0)

    def own_of(a, d):
        return part_of(mine, a, d) + below * part_of(met, a, d)

    @pl.when(step == 0)
    def _():
        spread(total, core, own_of)
        spread(total, 1 - core, functools.partial(part_of, other))
        coef[...] = jnp.broadcast_to(row_ref[...], (ROWS, ROWS)).T

    coefficient = coef[...]
    for tile in range(FINISH_WIDE // 128):
        span = slice(tile * 128, (tile + 1) * 128)
        first = pl.multiple_of(step * FINISH_WIDE + tile * 128, 128)
        top = coefficient * top_ref[:, span].astype(jnp.float32)
        out_ref[:, pl.ds(first, 128)] = top + total[pl.ds(first, 128), :].T


def base_terms(mine, met, other, top, coefficient):
    return pl.pallas_call(
        base_kernel,
        grid=(FINISH_STEPS,),
        out_shape=shape_of((ROWS, D), jnp.float32),
        in_specs=whole(6) + [pl.BlockSpec((ROWS, FINISH_WIDE), lambda step: (0, step))] + whole(1),
        out_specs=pl.BlockSpec(memory_space=pltpu.VMEM),
        scratch_shapes=[pltpu.VMEM((D, ROWS), jnp.float32), pltpu.VMEM((ROWS, ROWS), jnp.float32)],
        compiler_params=VMEM,
        cost_estimate=cost(0, 8 * 2**20),
        name="base_terms",
    )(*mine, *met, *other, top, coefficient)


def finish_kernel(*refs):
    wrap, down, swap, back_in = refs[:2], refs[2:4], refs[4:6], refs[6:8]
    base_ref, out_hbm, total, out_ref, sems = refs[8:]
    _, _, _, core = place()

    def upper_of(a, d):
        upper = part_of(wrap, a, d) + (part_of(down, a, d) + part_of(swap, a, d))
        return upper.astype(jnp.bfloat16)

    spread(total, core, upper_of)
    spread(total, 1 - core, lambda a, d: back_in[a // 2][a % 2, d])
    copies = []
    for step in range(FINISH_STEPS):
        for tile in range(step * FINISH_WIDE // 128, (step + 1) * FINISH_WIDE // 128):
            span = slice(tile * 128, (tile + 1) * 128)
            turned = total[span, :].T.astype(jnp.float32)
            out_ref[:, span] = (base_ref[:, span] + turned).astype(jnp.bfloat16)
        wide = slice(step * FINISH_WIDE, (step + 1) * FINISH_WIDE)
        copies += start_copies([out_ref.at[:, wide]], [out_hbm.at[:, wide]], sems.at[step:])
    for copy in copies:
        copy.wait()


def finish(wrap, down, swap, back_in, base):
    return pl.pallas_call(
        finish_kernel,
        out_shape=shape_of((ROWS, D)),
        in_specs=whole(9),
        out_specs=pl.BlockSpec(memory_space=pl.ANY),
        scratch_shapes=[
            pltpu.VMEM((D, ROWS), jnp.bfloat16),
            pltpu.VMEM((ROWS, D), jnp.bfloat16),
            pltpu.SemaphoreType.DMA((FINISH_STEPS,)),
        ],
        compiler_params=VMEM,
        cost_estimate=cost(0, 6 * 2**20),
        name="finish",
    )(*wrap, *down, *swap, *back_in, base)


def scatter_z(terms):
    wide = jnp.float32

    def add(first, second):
        return (first.astype(wide) + second.astype(wide)).astype(jnp.bfloat16)

    own, next_up, after_up, low_3, high_3, low_4, high_4, low_5, high_5, after_down, next_down = terms
    far_up, far_down = shift_z(low_4, 1), shift_z(high_4, -1)
    up = jnp.concatenate([add(low_3, far_up), high_3], axis=0)
    down = jnp.concatenate([low_5, add(high_5, far_down)], axis=0)
    up, down = shift_z(up, 1), shift_z(down, -1)
    up, down = add(after_up, up), add(after_down, down)
    up, down = shift_z(up, 1), shift_z(down, -1)
    up, down = add(next_up, up), add(next_down, down)
    return own, shift_z(up, 1), shift_z(down, -1)


def local(
    hidden_in,
    norm_gain,
    key_weight,
    value_weight,
    queries,
    stashed_keys,
    stashed_values,
    out_cotangent,
    logprob_grad,
    new_logprob,
    old_logprob,
    advantages,
    segment_ids,
):
    wide = jnp.float32
    _, _, y, core = place()
    half = SLAB // 2
    gain = norm_gain[0].astype(wide)[:, None]
    weight_pair = jnp.concatenate([key_weight[0], value_weight[0]], axis=1).astype(wide)
    own = (weight_pair * gain).astype(jnp.bfloat16)
    up_1, down_1 = shift_z(own, 1), shift_z(own, -1)

    cots, near, part_up, part_down = attend(
        hidden_in[0],
        segment_ids,
        stashed_keys[0],
        stashed_values[0],
        queries[0],
        out_cotangent[0],
    )
    met_up, met_down = shift_x(part_up, 1), shift_x(part_down, -1)
    up_2, down_2 = shift_z(up_1, 1), shift_z(down_1, -1)

    segments = after(segment_ids, up_1)[0]
    row_adv = jnp.zeros((ROWS,), wide)
    for index in range(advantages.shape[1]):
        row_adv = row_adv + jnp.where(segments == index, advantages[0, index], 0.0)
    ratio = jnp.exp(after(new_logprob, up_1) - old_logprob)
    coefficient = -jnp.clip(ratio, 0.8, 1.28) * row_adv
    up_2, down_2 = after((up_2, down_2), coefficient)

    up_3, down_3 = shift_z(up_2, 1), shift_z(down_2, -1)
    relay = slice(RELAY, RELAY + RELAYED)
    far_up, far_down = shift_x(met_up[relay], 1), shift_x(met_down[relay], -1)
    met = [cots, met_up, met_down, far_up, far_down]
    up_4, down_4 = shift_z(up_3[:half], 1), shift_z(down_3[half:], -1)

    opposite = jnp.concatenate([up_4, down_4], axis=0)
    products = back([own, down_1, up_1, down_2, up_2, down_3, up_3, opposite], met)
    met_late = after(met, products[0])
    products = [products[0]] + [shift_x(products[d], -d) for d in (1, 2, 3)]
    terms = weight_terms(near, met_late)
    sums = scatter_z(after(terms, products[1]))
    key_grad, value_grad = (
        gain * (sums[0][:, span].astype(wide) + (sums[1][:, span].astype(wide) + sums[2][:, span].astype(wide)))
        for span in (slice(0, KVW), slice(KVW, 2 * KVW))
    )

    *mine, other_a, other_b = local_terms(products, (near, part_up, part_down))
    other = [other_a, other_b]
    met_other = [swap_core(part) for part in other]
    pairs = [(own.astype(wide) + part.astype(wide)).astype(jnp.bfloat16) for own, part in zip(mine, met_other)]
    base = base_terms(mine, met_other, other, logprob_grad, after(coefficient[None], *pairs))
    wrap, down, swap, back_in = [], [], [], []
    for own, pair in zip(mine, pairs):
        wrap.append(send_y(pair, [(3, 0)]))
        down.append(send_y(pair, [(3, 2), (2, 1)]))
        if len(wrap) == 2:
            wrap[-1] = after(wrap[-1], base)
        onward = jnp.where(y == 0, wrap[-1].astype(wide), pair.astype(wide) + down[-1].astype(wide))
        swap.append(send_y(onward.astype(jnp.bfloat16), [(0, 1), (1, 0)]))
        upper = wrap[-1].astype(wide) + (down[-1].astype(wide) + swap[-1].astype(wide))
        upper = upper + jnp.where(core == 1, own.astype(wide), 0.0)
        back_in.append(swap_core(upper.astype(jnp.bfloat16)))
    hidden_cotangent = finish(wrap, down, swap, back_in, base)
    return hidden_cotangent[None], key_grad[None], value_grad[None]


def solution(mesh):
    return jax.shard_map(
        local,
        mesh=mesh,
        in_specs=(
            P("section", "dp", None),
            P("section", "dp"),
            P("section", "dp", None),
            P("section", "dp", None),
            P("section", "dp", None),
            P("section", "dp", None),
            P("section", "dp", None),
            P("section", "dp", None),
            P("dp", None),
            P("dp"),
            P("dp"),
            P("dp", None),
            P("dp", None),
        ),
        out_specs=(P("section", "dp", None), P("section", "dp", None), P("section", "dp", None)),
        check_vma=False,
    )
```

```python
import functools
import math

import jax
import jax.numpy as jnp
from jax import lax
from jax.experimental import pallas as pl
from jax.experimental.pallas import tpu as pltpu
from jax.sharding import PartitionSpec as P

D = 5120
HD = 128
KVH = 4
GROUP = 8
KVW = 512
ROWS = 128
NZ = 8
NX = 4
NY = 4
SLAB = D // (NZ * NX)
EPSILON = 1e-06
VMEM = pltpu.CompilerParams(vmem_limit_bytes=12 * 1024 * 1024)
MOST_VMEM = pltpu.CompilerParams(vmem_limit_bytes=57 * 1024 * 1024)
NT = (((1,), (1,)), ((), ()))

Z_ORDER = (0, 1, 7, 2, 6, 3, 5, 4)
HALVED = (3, 4, 5)
TERM_ROWS = [SLAB] * 3 + [SLAB // 2] * 6 + [SLAB] * 2
COTS = 2 * KVW // 128
STREAM = NZ * SLAB
RELAY = STREAM
RELAYED = NZ // 2 * SLAB + COTS // 2 * ROWS
SENT = RELAY + RELAYED + COTS // 2 * ROWS


def shape_of(shape, dtype=jnp.bfloat16):
    return jax.ShapeDtypeStruct(shape, dtype)


def whole(count):
    return [pl.BlockSpec(memory_space=pltpu.VMEM)] * count


def after(values, *first):
    return lax.optimization_barrier((values, first))[0]


def cost(flops, moved, exps=0):
    return pl.CostEstimate(flops=flops, bytes_accessed=moved, transcendentals=exps)


def shift_z(value, step):
    pairs = [(z * NX + x, ((z + step) % NZ) * NX + x) for z in range(NZ) for x in range(NX)]
    return lax.ppermute(value, "dp", pairs)


def shift_x(value, step):
    pairs = [(z * NX + x, z * NX + (x + step) % NX) for z in range(NZ) for x in range(NX)]
    return lax.ppermute(value, "dp", pairs)


def swap_core(value):
    return lax.ppermute(value, "section", [(s, s ^ 1) for s in range(2 * NY)])


def send_y(value, routes):
    pairs = [(2 * a + c, 2 * b + c) for a, b in routes for c in range(2)]
    return lax.ppermute(value, "section", pairs)


def place():
    own = lax.axis_index("dp")
    layer = lax.axis_index("section")
    return own // NX, own % NX, layer // 2, layer % 2


def start_copies(sources, targets, sems):
    copies = [
        pltpu.make_async_copy(source, target, sems.at[index])
        for index, (source, target) in enumerate(zip(sources, targets))
    ]
    for copy in copies:
        copy.start()
    return copies


def attend_kernel(*refs):
    (h_hbm, row_hbm, k_hbm, v_hbm, q_hbm, o_hbm), (cots_out, near_out, up_out, down_out) = refs[:6], refs[6:10]
    h_ref, row_ref, k_ref, v_ref, q_ref, o_ref, held, tiles, in_sems, out_sems = refs[10:]
    pieces = [
        (hbm.at[:, first : first + wide], ref.at[:, first : first + wide])
        for hbm, ref, wide in ((h_hbm, h_ref, D // 4),)
        for first in range(0, D, wide)
    ]
    pieces += [(row_hbm, row_ref), (k_hbm, k_ref), (v_hbm, v_ref)]
    for g in range(KVH):
        span = slice(g * GROUP * HD, (g + 1) * GROUP * HD)
        pieces += [(q_hbm.at[:, span], q_ref.at[:, span]), (o_hbm.at[:, span], o_ref.at[:, span])]
    copies = start_copies([pair[0] for pair in pieces], [pair[1] for pair in pieces], in_sems)
    z, x, _, _ = place()
    squares = jnp.zeros((ROWS, 128), jnp.float32)
    for tile in range(D // 128):
        if tile % 10 == 0:
            copies[tile // 10].wait()
        part = h_ref[:, tile * 128 : (tile + 1) * 128]
        turned = part.T
        part = part.astype(jnp.float32)
        squares = squares + part * part
        for piece in range(4):
            unit = tile * 4 + piece
            slab, fifth = unit // 5, unit % 5
            k = lax.rem(slab // NX - z + NZ, NZ)
            d = lax.rem(slab % NX - x + NX, NX)
            first = pl.multiple_of(k * SLAB + fifth * 32, 32)
            held[d, pl.ds(first, 32), :] = turned[piece * 32 : (piece + 1) * 32, :]
    middle = STREAM // 2
    sent = start_copies(
        [held.at[0], held.at[1], held.at[2, :middle], held.at[3], held.at[2, middle:]],
        [
            near_out,
            up_out.at[:STREAM],
            up_out.at[STREAM : STREAM + middle],
            down_out.at[:STREAM],
            down_out.at[STREAM : STREAM + middle],
        ],
        out_sems,
    )
    inv_rms = lax.rsqrt(jnp.sum(squares, axis=1, keepdims=True) * (1.0 / D) + EPSILON)
    for copy in copies[4:7]:
        copy.wait()
    j_place = lax.broadcasted_iota(jnp.int32, (ROWS, ROWS), 0)
    i_place = lax.broadcasted_iota(jnp.int32, (ROWS, ROWS), 1)
    segment = jnp.broadcast_to(row_ref[...].astype(jnp.float32), (ROWS, ROWS))
    allowed = (segment.T == segment) & (j_place <= i_place)
    scale = 1.0 / math.sqrt(HD)
    for g in range(KVH):
        for copy in copies[7 + 2 * g : 9 + 2 * g]:
            copy.wait()
        key = k_ref[:, g * HD : (g + 1) * HD]
        value = v_ref[:, g * HD : (g + 1) * HD]
        heads = range(g * GROUP, (g + 1) * GROUP)
        query = jnp.concatenate([q_ref[:, n * HD : (n + 1) * HD] for n in heads], axis=0)
        cot = jnp.concatenate([o_ref[:, n * HD : (n + 1) * HD] for n in heads], axis=0)
        scores = lax.dot_general(key, query, NT, preferred_element_type=jnp.float32) * scale
        prob_cot = lax.dot_general(value, cot, NT, preferred_element_type=jnp.float32)
        halves, cots = [], []
        for n in range(GROUP):
            span = slice(n * ROWS, (n + 1) * ROWS)
            score = jnp.where(allowed, scores[:, span], -jnp.inf)
            high = jnp.max(score, axis=0, keepdims=True)
            grown = jnp.exp(score - high)
            probs = grown * (1.0 / jnp.sum(grown, axis=0, keepdims=True))
            half = probs.astype(jnp.bfloat16)
            pulled = prob_cot[:, span]
            delta = jnp.sum(half.astype(jnp.float32) * pulled, axis=0, keepdims=True)
            halves.append(half)
            cots.append((probs * (pulled - delta)).astype(jnp.bfloat16))
        key_cot = jnp.dot(jnp.concatenate(cots, axis=1), query, preferred_element_type=jnp.float32)
        value_cot = jnp.dot(jnp.concatenate(halves, axis=1), cot, preferred_element_type=jnp.float32)
        key_cot = (key_cot * scale).astype(jnp.bfloat16).astype(jnp.float32)
        value_cot = value_cot.astype(jnp.bfloat16).astype(jnp.float32)
        for index, value in ((g, key_cot), (KVH + g, value_cot)):
            tiles[index * ROWS : (index + 1) * ROWS, :] = (value * inv_rms).astype(jnp.bfloat16)
    part, lead = COTS // 2 * ROWS, STREAM + STREAM // 2
    sent += start_copies(
        [tiles, tiles, tiles.at[part:], tiles.at[:part]],
        [cots_out, up_out.at[lead:], down_out.at[lead : lead + part], down_out.at[lead + part :]],
        out_sems.at[5:],
    )
    for copy in sent:
        copy.wait()


def attend(hidden, row, keys, values, queries, cotangent):
    operands = (hidden, row, keys, values, queries, cotangent)
    return pl.pallas_call(
        attend_kernel,
        out_shape=[shape_of((COTS * ROWS, ROWS)), shape_of((STREAM, ROWS)), shape_of((SENT, ROWS)), shape_of((SENT, ROWS))],
        in_specs=[pl.BlockSpec(memory_space=pl.ANY)] * 6,
        out_specs=[pl.BlockSpec(memory_space=pl.ANY)] * 4,
        scratch_shapes=[pltpu.VMEM(a.shape, a.dtype) for a in operands]
        + [
            pltpu.VMEM((NX, STREAM, ROWS), jnp.bfloat16),
            pltpu.VMEM((COTS * ROWS, ROWS), jnp.bfloat16),
            pltpu.SemaphoreType.DMA((15,)),
            pltpu.SemaphoreType.DMA((9,)),
        ],
        compiler_params=MOST_VMEM,
        cost_estimate=cost(4 * 32 * 2 * 128**3, 4 * 2**20, 32 * 128 * 128),
        name="attend",
    )(*operands)


def join_cots(cots, up, down, far_up, far_down, right):
    lead, far = SENT - COTS * ROWS, RELAYED - COTS // 2 * ROWS
    for tile in range(COTS):
        span = slice(tile * 128, (tile + 1) * 128)
        right[:ROWS, span] = cots[tile * ROWS : (tile + 1) * ROWS]
        first = lead + tile * ROWS
        right[ROWS : 2 * ROWS, span] = up[first : first + ROWS]
        source, first = (far_up, far + tile * ROWS) if tile < COTS // 2 else (far_down, far + (tile - COTS // 2) * ROWS)
        right[2 * ROWS : 3 * ROWS, span] = source[first : first + ROWS]
        first = lead + (tile + COTS // 2) % COTS * ROWS
        right[3 * ROWS :, span] = down[first : first + ROWS]


def grad_kernel(near, cots, up, down, far_up, far_down, *refs):
    outs, (left, right) = refs[:-2], refs[-2:]
    join_cots(cots, up, down, far_up, far_down, right)
    middle = NZ // 2 * SLAB
    left[:, :ROWS] = near[...]
    left[:, ROWS : 2 * ROWS] = up[: NZ * SLAB]
    left[:middle, 2 * ROWS : 3 * ROWS] = far_up[:middle]
    left[middle:, 2 * ROWS : 3 * ROWS] = far_down[:middle]
    left[:, 3 * ROWS :] = down[: NZ * SLAB]
    place_k, half = 0, SLAB // 2
    for k in range(NZ):
        term = jnp.dot(
            left[k * SLAB : (k + 1) * SLAB], right[...], preferred_element_type=jnp.float32
        ).astype(jnp.bfloat16)
        if k in HALVED:
            outs[place_k][...] = term[:half]
            outs[place_k + 1][...] = term[half:]
        else:
            outs[place_k][...] = term
        place_k += 2 if k in HALVED else 1


def weight_terms(near, met):
    return pl.pallas_call(
        grad_kernel,
        out_shape=[shape_of((rows, 2 * KVW)) for rows in TERM_ROWS],
        in_specs=whole(6),
        out_specs=whole(len(TERM_ROWS)),
        scratch_shapes=[
            pltpu.VMEM((NZ * SLAB, NX * ROWS), jnp.bfloat16),
            pltpu.VMEM((NX * ROWS, 2 * KVW), jnp.bfloat16),
        ],
        compiler_params=VMEM,
        cost_estimate=cost(2 * 512 * 1280 * 1024, 6 * 2**20),
        name="weight_terms",
    )(near, *met)


def back_kernel(*refs):
    weights, cots, outs, right = refs[:NZ], refs[NZ : NZ + 5], refs[NZ + 5 : -1], refs[-1]
    join_cots(*cots, right)
    for place_k, weight in enumerate(weights):
        full = lax.dot_general(weight[...], right[...], NT, preferred_element_type=jnp.float32)
        for d in range(NX):
            outs[d][place_k] = full[:, d * ROWS : (d + 1) * ROWS].astype(jnp.bfloat16)


def back(weights, cots):
    return pl.pallas_call(
        back_kernel,
        out_shape=[shape_of((NZ, SLAB, ROWS))] * NX,
        in_specs=whole(NZ + 5),
        out_specs=whole(NX),
        scratch_shapes=[pltpu.VMEM((NX * ROWS, 2 * KVW), jnp.bfloat16)],
        compiler_params=VMEM,
        cost_estimate=cost(2 * 512 * 1280 * 1024, 2**20 * 5),
        name="back",
    )(*weights, *cots)


def local_kernel(*refs):
    products, (near, up, down) = refs[:NX], refs[NX : NX + 3]
    mine, other, held = refs[NX + 3 : NX + 5], refs[NX + 5 : NX + 7], refs[-1]

    def stream_of(d, k):
        if d == 0:
            part = near[k * SLAB : (k + 1) * SLAB]
        else:
            source = (None, up, up if k < NZ // 2 else down, down)[d]
            first = RELAY + k % (NZ // 2) * SLAB if d == 2 else k * SLAB
            part = source[first : first + SLAB, :]
        return part.astype(jnp.float32)

    _, _, _, core = place()
    squares = jnp.zeros((SLAB, ROWS), jnp.float32)
    along = jnp.zeros((SLAB, ROWS), jnp.float32)
    for d in range(NX):
        for place_k, k in enumerate(Z_ORDER):
            stream = stream_of(d, k)
            squares = squares + stream * stream
            along = along + stream * products[d][place_k].astype(jnp.float32)
    inv_rms = lax.rsqrt(jnp.sum(squares, axis=0, keepdims=True) * (1.0 / D) + EPSILON)
    pull = inv_rms * inv_rms * (jnp.sum(along, axis=0, keepdims=True) * (1.0 / D))
    for d in range(NX):
        for place_k, k in enumerate(Z_ORDER):
            stream = stream_of(d, k)
            term = products[d][place_k].astype(jnp.float32) - stream * pull
            held[k // 4, k % 4, d] = term.astype(jnp.bfloat16)
    for chunk in range(2):
        mine[chunk][...] = held[core, 2 * chunk : 2 * chunk + 2]
        other[chunk][...] = held[1 - core, 2 * chunk : 2 * chunk + 2]


def local_terms(products, turned):
    return pl.pallas_call(
        local_kernel,
        out_shape=[shape_of((2, NX, SLAB, ROWS))] * 4,
        in_specs=whole(NX + 3),
        out_specs=whole(4),
        scratch_shapes=[pltpu.VMEM((2, 4, NX, SLAB, ROWS), jnp.bfloat16)],
        compiler_params=VMEM,
        cost_estimate=cost(0, 4 * 2**20),
        name="local_terms",
    )(*products, *turned)


FINISH_STEPS = 5
FINISH_WIDE = D // FINISH_STEPS


def spread(total, half, value_of):
    z, x, _, _ = place()
    for a in range(4):
        for d in range(NX):
            slab = lax.rem(z + half * 4 + a, NZ) * NX + lax.rem(x + d, NX)
            total[pl.ds(pl.multiple_of(slab * SLAB, 32), SLAB), :] = value_of(a, d)


def part_of(chunks, a, d):
    return chunks[a // 2][a % 2, d].astype(jnp.float32)


def base_kernel(*refs):
    mine, met, other = refs[:2], refs[2:4], refs[4:6]
    top_ref, row_ref, out_ref, total, coef = refs[6:]
    _, _, _, core = place()
    below = (1 - core).astype(jnp.float32)
    step = pl.program_id(0)

    def own_of(a, d):
        return part_of(mine, a, d) + below * part_of(met, a, d)

    @pl.when(step == 0)
    def _():
        spread(total, core, own_of)
        spread(total, 1 - core, functools.partial(part_of, other))
        coef[...] = jnp.broadcast_to(row_ref[...], (ROWS, ROWS)).T

    coefficient = coef[...]
    for tile in range(FINISH_WIDE // 128):
        span = slice(tile * 128, (tile + 1) * 128)
        first = pl.multiple_of(step * FINISH_WIDE + tile * 128, 128)
        top = coefficient * top_ref[:, span].astype(jnp.float32)
        out_ref[:, pl.ds(first, 128)] = top + total[pl.ds(first, 128), :].T


def base_terms(mine, met, other, top, coefficient):
    return pl.pallas_call(
        base_kernel,
        grid=(FINISH_STEPS,),
        out_shape=shape_of((ROWS, D), jnp.float32),
        in_specs=whole(6) + [pl.BlockSpec((ROWS, FINISH_WIDE), lambda step: (0, step))] + whole(1),
        out_specs=pl.BlockSpec(memory_space=pltpu.VMEM),
        scratch_shapes=[pltpu.VMEM((D, ROWS), jnp.float32), pltpu.VMEM((ROWS, ROWS), jnp.float32)],
        compiler_params=VMEM,
        cost_estimate=cost(0, 8 * 2**20),
        name="base_terms",
    )(*mine, *met, *other, top, coefficient)


def finish_kernel(*refs):
    wrap, down, swap, back_in = refs[:2], refs[2:4], refs[4:6], refs[6:8]
    base_ref, out_hbm, total, out_ref, sems = refs[8:]
    _, _, _, core = place()

    def upper_of(a, d):
        upper = part_of(wrap, a, d) + (part_of(down, a, d) + part_of(swap, a, d))
        return upper.astype(jnp.bfloat16)

    spread(total, core, upper_of)
    spread(total, 1 - core, lambda a, d: back_in[a // 2][a % 2, d])
    copies = []
    for step in range(FINISH_STEPS):
        for tile in range(step * FINISH_WIDE // 128, (step + 1) * FINISH_WIDE // 128):
            span = slice(tile * 128, (tile + 1) * 128)
            turned = total[span, :].T.astype(jnp.float32)
            out_ref[:, span] = (base_ref[:, span] + turned).astype(jnp.bfloat16)
        wide = slice(step * FINISH_WIDE, (step + 1) * FINISH_WIDE)
        copies += start_copies([out_ref.at[:, wide]], [out_hbm.at[:, wide]], sems.at[step:])
    for copy in copies:
        copy.wait()


def finish(wrap, down, swap, back_in, base):
    return pl.pallas_call(
        finish_kernel,
        out_shape=shape_of((ROWS, D)),
        in_specs=whole(9),
        out_specs=pl.BlockSpec(memory_space=pl.ANY),
        scratch_shapes=[
            pltpu.VMEM((D, ROWS), jnp.bfloat16),
            pltpu.VMEM((ROWS, D), jnp.bfloat16),
            pltpu.SemaphoreType.DMA((FINISH_STEPS,)),
        ],
        compiler_params=VMEM,
        cost_estimate=cost(0, 6 * 2**20),
        name="finish",
    )(*wrap, *down, *swap, *back_in, base)


def scatter_z(terms):
    wide = jnp.float32

    def add(first, second):
        return (first.astype(wide) + second.astype(wide)).astype(jnp.bfloat16)

    own, next_up, after_up, low_3, high_3, low_4, high_4, low_5, high_5, after_down, next_down = terms
    far_up, far_down = shift_z(low_4, 1), shift_z(high_4, -1)
    up = jnp.concatenate([add(low_3, far_up), high_3], axis=0)
    down = jnp.concatenate([low_5, add(high_5, far_down)], axis=0)
    up, down = shift_z(up, 1), shift_z(down, -1)
    up, down = add(after_up, up), add(after_down, down)
    up, down = shift_z(up, 1), shift_z(down, -1)
    up, down = add(next_up, up), add(next_down, down)
    return own, shift_z(up, 1), shift_z(down, -1)


def local(
    hidden_in,
    norm_gain,
    key_weight,
    value_weight,
    queries,
    stashed_keys,
    stashed_values,
    out_cotangent,
    logprob_grad,
    new_logprob,
    old_logprob,
    advantages,
    segment_ids,
):
    wide = jnp.float32
    _, _, y, core = place()
    half = SLAB // 2
    gain = norm_gain[0].astype(wide)[:, None]
    weight_pair = jnp.concatenate([key_weight[0], value_weight[0]], axis=1).astype(wide)
    own = (weight_pair * gain).astype(jnp.bfloat16)
    up_1, down_1 = shift_z(own, 1), shift_z(own, -1)

    cots, near, part_up, part_down = attend(
        hidden_in[0],
        segment_ids,
        stashed_keys[0],
        stashed_values[0],
        queries[0],
        out_cotangent[0],
    )
    met_up, met_down = shift_x(part_up, 1), shift_x(part_down, -1)
    up_2, down_2 = shift_z(up_1, 1), shift_z(down_1, -1)

    segments = after(segment_ids, up_1)[0]
    row_adv = jnp.zeros((ROWS,), wide)
    for index in range(advantages.shape[1]):
        row_adv = row_adv + jnp.where(segments == index, advantages[0, index], 0.0)
    ratio = jnp.exp(after(new_logprob, up_1) - old_logprob)
    coefficient = -jnp.clip(ratio, 0.8, 1.28) * row_adv
    up_2, down_2 = after((up_2, down_2), coefficient)

    up_3, down_3 = shift_z(up_2, 1), shift_z(down_2, -1)
    relay = slice(RELAY, RELAY + RELAYED)
    far_up, far_down = shift_x(met_up[relay], 1), shift_x(met_down[relay], -1)
    met = [cots, met_up, met_down, far_up, far_down]
    up_4, down_4 = shift_z(up_3[:half], 1), shift_z(down_3[half:], -1)

    opposite = jnp.concatenate([up_4, down_4], axis=0)
    products = back([own, down_1, up_1, down_2, up_2, down_3, up_3, opposite], met)
    met_late = after(met, products[0])
    products = [products[0]] + [shift_x(products[d], -d) for d in (1, 2, 3)]
    terms = weight_terms(near, met_late)
    sums = scatter_z(after(terms, products[1]))
    key_grad, value_grad = (
        gain * (sums[0][:, span].astype(wide) + (sums[1][:, span].astype(wide) + sums[2][:, span].astype(wide)))
        for span in (slice(0, KVW), slice(KVW, 2 * KVW))
    )

    *mine, other_a, other_b = local_terms(products, (near, part_up, part_down))
    other = [other_a, other_b]
    met_other = [swap_core(part) for part in other]
    pairs = [(own.astype(wide) + part.astype(wide)).astype(jnp.bfloat16) for own, part in zip(mine, met_other)]
    base = base_terms(mine, met_other, other, logprob_grad, after(coefficient[None], *pairs))
    wrap, down, swap, back_in = [], [], [], []
    for own, pair in zip(mine, pairs):
        wrap.append(send_y(pair, [(3, 0)]))
        down.append(send_y(pair, [(3, 2), (2, 1)]))
        if len(wrap) == 2:
            wrap[-1] = after(wrap[-1], base)
        onward = jnp.where(y == 0, wrap[-1].astype(wide), pair.astype(wide) + down[-1].astype(wide))
        swap.append(send_y(onward.astype(jnp.bfloat16), [(0, 1), (1, 0)]))
        upper = wrap[-1].astype(wide) + (down[-1].astype(wide) + swap[-1].astype(wide))
        upper = upper + jnp.where(core == 1, own.astype(wide), 0.0)
        back_in.append(swap_core(upper.astype(jnp.bfloat16)))
    hidden_cotangent = finish(wrap, down, swap, back_in, base)
    return hidden_cotangent[None], key_grad[None], value_grad[None]


def solution(mesh):
    return jax.shard_map(
        local,
        mesh=mesh,
        in_specs=(
            P("section", "dp", None),
            P("section", "dp"),
            P("section", "dp", None),
            P("section", "dp", None),
            P("section", "dp", None),
            P("section", "dp", None),
            P("section", "dp", None),
            P("section", "dp", None),
            P("dp", None),
            P("dp"),
            P("dp"),
            P("dp", None),
            P("dp", None),
        ),
        out_specs=(P("section", "dp", None), P("section", "dp", None), P("section", "dp", None)),
        check_vma=False,
    )
```
